512 devices in a mesh: row: 16 (over y, core), col: 32 (over z, x).
Axes of the slice: x: 4, y: 8, z: 8, core: 2. Of those that a mesh axis runs over, the one named last changes fastest.
Arguments:
- covariance: float32 [2, 8192, 1, 16384], P(None, 'row', None, 'col'), may hold values from 0 to 11, as said below
Outputs:
- factored: float32 [2, 8192, 1, 16384], P(None, 'row', None, 'col')
The draws below stay inside these ranges and needn't reach their ends.
Inputs may be any that keep to these rules, and one draw needn't show every extreme that they name: covariance read as a matrix of order 16384 is exactly symmetric and positive definite, with positive entries.
All inputs are finite; a program needn't handle non-finite values.
Results may differ from the reference program's by a relative error of at most 0.000065.
Values sent between devices are 32-bit elements; how exact they have to be, the bound alone decides.
No kernel may reach another device: no remote copies, remote signals or barrier semaphores. Data moves between devices by JAX's collectives and lax.ppermute only.
A program may use at most 64 MiB of HBM per device.

```python
import jax
import jax.numpy as jnp
from jax import lax

TB = 512
TR_DEV = 2
TC_DEV = 1
NT = 32


def draw_covariance(key, part):
    key = jax.random.fold_in(key, 7)
    place_key, scale_key = jax.random.split(key)
    count = NT * TB
    places = jax.random.uniform(place_key, (count, 2), jnp.float32)
    scales = jnp.exp(jax.random.uniform(scale_key, (count,), jnp.float32, -0.5, 0.5))
    delta_x = places[:, 0][:, None] - places[:, 0][None, :]
    delta_y = places[:, 1][:, None] - places[:, 1][None, :]
    distance = jnp.sqrt(delta_x * delta_x + delta_y * delta_y)
    kernel = jnp.exp(-distance / 0.1)
    index = jnp.arange(count, dtype=jnp.int32)
    nugget = jnp.where(index[:, None] == index[None, :], 0.2, 0.0)
    matrix = scales[:, None] * scales[None, :] * (kernel + nugget)
    return matrix.reshape(TR_DEV, count // TR_DEV, TC_DEV, count // TC_DEV).astype(jnp.float32)


def setup_inputs(seed: int = 0) -> dict:
    keys = jax.random.split(jax.random.key(seed), 2)
    covariance = draw_covariance(jax.random.fold_in(keys[1], 71), 0)
    return {"covariance": covariance}


def reference(covariance):
    order = covariance.shape[0] * covariance.shape[1]
    matrix = covariance.reshape(order, order)
    factor = jnp.linalg.cholesky(matrix[:TB, :TB])
    solved = jax.scipy.linalg.solve_triangular(factor, matrix[:, :TB].T, lower=True).T
    panel = jnp.concatenate([factor, solved[TB:]], axis=0)
    updated = matrix - jnp.dot(panel.astype(jnp.float32), panel.T.astype(jnp.float32), preferred_element_type=jnp.float32, precision=lax.Precision.HIGHEST)
    tile_index = jnp.arange(order, dtype=jnp.int32) // TB
    lower = tile_index[:, None] >= tile_index[None, :]
    result = jnp.where(lower, updated, matrix)
    result = jnp.concatenate([panel, result[:, TB:]], axis=1)
    return result.reshape(covariance.shape)
```

```python
import functools

import jax
import jax.numpy as jnp
from jax import lax
from jax.experimental import pallas as pl
from jax.experimental.pallas import tpu as pltpu
from jax.sharding import PartitionSpec as P

AXES = ("row", "col")
ROWS, COLS = 16, 32
NY, NZ, NX = 8, 8, 4
TB = 512
SB = 128
HB = 256
SLOTS = 12
HIGHEST = lax.Precision.HIGHEST
M0, M1, X10, L20, L21, L30, L31, M2, M3, X32 = range(10)


def nn(a, b):
    return lax.dot_general(a, b, (((1,), (0,)), ((), ())), precision=HIGHEST, preferred_element_type=jnp.float32)


def nt(a, b):
    return lax.dot_general(a, b, (((1,), (1,)), ((), ())), precision=HIGHEST, preferred_element_type=jnp.float32)


def factor_block(block):
    tiles = SB // 8
    lane = lax.broadcasted_iota(jnp.int32, (8, SB), 1)
    sub = lax.broadcasted_iota(jnp.int32, (8, SB), 0)
    s = [block[8 * t : 8 * t + 8, :] for t in range(tiles)]
    e = [jnp.where(lane == sub + 8 * t, 1.0, 0.0).astype(jnp.float32) for t in range(tiles)]
    upper, inverse = [], []
    for b in range(tiles):
        cols = [
            [jnp.broadcast_to(s[t][:, 8 * b + m : 8 * b + m + 1], (8, SB)) for t in range(b, tiles)]
            for m in range(8)
        ]
        top, top_e = s[b], e[b]
        out_u, out_e = jnp.zeros_like(top), jnp.zeros_like(top)
        done = []
        for m in range(8):
            d = jnp.broadcast_to(cols[m][0][m : m + 1, :], (8, SB))
            r = lax.rsqrt(d)
            r = r * (1.5 - (0.5 * d) * (r * r))
            lc = [c * r for c in cols[m]]
            ur = jnp.broadcast_to(top[m : m + 1, :], (8, SB)) * r
            er = jnp.broadcast_to(top_e[m : m + 1, :], (8, SB)) * r
            out_u = jnp.where(sub == m, ur, out_u)
            out_e = jnp.where(sub == m, er, out_e)
            for k in range(m + 1, 8):
                f = jnp.broadcast_to(lc[0][k : k + 1, :], (8, SB))
                cols[k] = [c - l * f for c, l in zip(cols[k], lc)]
            below = jnp.where(sub > m, lc[0], 0.0)
            top = top - below * ur
            top_e = top_e - below * er
            done.append((lc, ur, er))
        for t in range(b + 1, tiles):
            for lc, ur, er in done:
                s[t] = s[t] - lc[t - b] * ur
                e[t] = e[t] - lc[t - b] * er
        upper.append(jnp.where(lane >= sub + 8 * b, out_u, 0.0))
        inverse.append(out_e)
    return jnp.concatenate(upper, axis=0), jnp.concatenate(inverse, axis=0)


def factor_kernel(k, flag_ref, w_in, f_in, w_ref, f_ref):
    @pl.when(flag_ref[0] == 1)
    def _():
        lo, hi = k * SB, (k + 1) * SB
        w_ref[...] = w_in[...]
        f_ref[...] = f_in[...]

        def slot(i):
            return pl.ds(i * SB, SB)

        u, inv = factor_block(w_in[lo:hi, lo:hi])
        f_ref[slot((M0, M1, M2, M3)[k]), :] = inv
        w_ref[lo:hi, lo:hi] = u.T
        if k % 2 == 1:
            prev = f_in[slot((M0, M2)[k // 2]), :]
            f_ref[slot((X10, X32)[k // 2]), :] = -nn(inv, nn(w_in[lo:hi, lo - SB : lo], prev))
        if hi < TB:
            below = nt(w_in[hi:, lo:hi], inv)
            w_ref[hi:, lo:hi] = below
            w_ref[lo:hi, hi:] = jnp.zeros((SB, TB - hi), jnp.float32)
            w_ref[hi:, hi:] = w_in[hi:, hi:] - nt(below, below)
            if k < 2:
                f_ref[slot((L20, L21)[k]), :] = below[2 * SB - hi : 3 * SB - hi]
                f_ref[slot((L30, L31)[k]), :] = below[3 * SB - hi : 4 * SB - hi]


def factor_step(k, flag, w, f):
    vmem = pl.BlockSpec(memory_space=pltpu.VMEM)
    return pl.pallas_call(
        functools.partial(factor_kernel, k),
        out_shape=(
            jax.ShapeDtypeStruct((TB, TB), jnp.float32),
            jax.ShapeDtypeStruct((SLOTS * SB, SB), jnp.float32),
        ),
        in_specs=[pl.BlockSpec(memory_space=pltpu.SMEM), vmem, vmem],
        out_specs=(vmem, vmem),
        cost_estimate=pl.CostEstimate(flops=8_000_000_000, bytes_accessed=3_000_000, transcendentals=0),
        compiler_params=pltpu.CompilerParams(vmem_limit_bytes=24 * 1024 * 1024),
        name=f"factor_{k}",
    )(flag, w, f)


def update_kernel(pos_ref, own_ref, left_ref, right_ref, opp_a_ref, opp_b_ref, b_ref, f_ref, w_ref, cov_ref, out_ref, y_ref):
    row, col, x = pos_ref[0], pos_ref[1], pos_ref[2]

    def block(i):
        place = lax.rem(i // 3 - x + 4, 4)
        return f_ref[pl.ds(pl.multiple_of(place * (3 * SB) + (i % 3) * SB, SB), SB), :]

    zero = jnp.zeros((SB, SB), jnp.float32)

    def square(a, b, c, d):
        return jnp.concatenate(
            [jnp.concatenate([a, b], axis=1), jnp.concatenate([c, d], axis=1)], axis=0
        )

    d0 = square(block(M0), zero, block(X10), block(M1))
    d1 = square(block(M2), zero, block(X32), block(M3))
    g = square(block(L20), block(L21), block(L30), block(L31))
    y0 = nn(d0, b_ref[0:HB, :])
    y_ref[0:HB, :] = y0
    y_ref[HB:TB, :] = nn(d1, b_ref[HB:TB, :] - nn(g, y0))

    opp = jnp.concatenate([opp_a_ref[...], opp_b_ref[...]], axis=0)
    pieces = ((0, own_ref[...]), (3, left_ref[...]), (1, right_ref[...]), (2, opp))
    for shift, raw in pieces:
        q = lax.rem(x + shift, 4)
        rows = pl.ds(pl.multiple_of(q * HB, HB), HB)
        x0 = nt(raw[:, 0:HB], d0)
        x1 = nt(raw[:, HB:TB] - nt(x0, g), d1)
        cov = cov_ref[rows, :]
        new = cov - (nn(x0, y_ref[0:HB, :]) + nn(x1, y_ref[HB:TB, :]))
        tile_row = row + ROWS * (q // 2)
        out = jnp.where(tile_row >= col, new, cov)
        out = jnp.where(col == 0, jnp.concatenate([x0, x1], axis=1), out)
        half = pl.ds(pl.multiple_of(lax.rem(q, 2) * HB, HB), HB)
        out_ref[rows, :] = jnp.where(jnp.logical_and(col == 0, tile_row == 0), w_ref[half, :], out)


def update(pos, own, left, right, opp_a, opp_b, b, f, w, cov):
    vmem = pl.BlockSpec(memory_space=pltpu.VMEM)
    return pl.pallas_call(
        update_kernel,
        out_shape=jax.ShapeDtypeStruct((2 * TB, TB), jnp.float32),
        in_specs=[pl.BlockSpec(memory_space=pltpu.SMEM)] + [vmem] * 9,
        out_specs=vmem,
        scratch_shapes=[pltpu.VMEM((TB, TB), jnp.float32)],
        cost_estimate=pl.CostEstimate(flops=8_000_000_000, bytes_accessed=9_000_000, transcendentals=0),
        compiler_params=pltpu.CompilerParams(vmem_limit_bytes=40 * 1024 * 1024),
        name="update",
    )(pos, own, left, right, opp_a, opp_b, b, f, w, cov)


def device(y, core, z, x):
    return (y * 2 + core) * COLS + z * NX + x


def send(value, pairs):
    return lax.ppermute(value, AXES, pairs)


def one_of(pos, places):
    found = pos == places[0]
    for place in places[1:]:
        found = jnp.logical_or(found, pos == place)
    return found


ROUNDS = (
    (((0, 3),), ((0, 5),)),
    (((0, 1), (3, 4), (5, 6)), ((0, 7), (3, 2))),
)


def ring_sends(value, moves, lift):
    return [send(value, [p for a, b in pairs for p in lift(a, b)]) for pairs in moves]


def ring_pick(value, moves, pos, got):
    for pairs, received in zip(moves, got):
        value = jnp.where(one_of(pos, [b for _, b in pairs]), received, value)
    return value


def ring_round(value, moves, pos, lift):
    return ring_pick(value, moves, pos, ring_sends(value, moves, lift))


def on_device(covariance):
    row = lax.axis_index("row")
    col = lax.axis_index("col")
    y, core = row // 2, row % 2
    z, x = col // NX, col % NX
    cov = lax.optimization_barrier(covariance.reshape(2 * TB, TB))
    is_root = jnp.logical_and(row == 0, col == 0)
    flag = is_root.astype(jnp.int32).reshape(1)
    everywhere = [(a, c) for a in range(NY) for c in range(2)]

    quarter = [cov[HB * q : HB * (q + 1)] for q in range(4)]
    got = [
        send(quarter[q], [(device(a, c, 0, 0), device(a, c, 0, q)) for a, c in everywhere])
        for q in (1, 3, 2)
    ]

    def along_z(a, b):
        xs = range(NX) if a < 4 and b < 4 else (2, 3)
        return [(device(i, c, a, j), device(i, c, b, j)) for i, c in everywhere for j in xs]

    def along_y(a, b):
        return [(device(a, 0, k, j), device(b, 0, k, j)) for k in range(NZ) for j in range(NX)]

    w, f = cov[0:TB], jnp.zeros((SLOTS * SB, SB), jnp.float32)
    b_tile = cov[0:TB]

    w, f = factor_step(0, flag, w, f)
    w, f = factor_step(1, flag, w, f)
    moved = ring_sends(b_tile, ROUNDS[0], along_y)
    w, f, got, moved = lax.optimization_barrier((w, f, got, moved))
    own = jnp.where(x == 0, quarter[0], jnp.where(x == 1, got[0], jnp.where(x == 2, got[2], got[1])))
    b_tile = ring_pick(b_tile, ROUNDS[0], y, moved)

    w, f = factor_step(2, flag, w, f)
    w, f = factor_step(3, flag, w, f)
    got = ring_sends(own, ROUNDS[0], along_z)
    moved = ring_sends(b_tile, ROUNDS[1], along_y)
    w, f, got, moved = lax.optimization_barrier((w, f, got, moved))
    own = ring_pick(own, ROUNDS[0], z, got)
    b_tile = ring_pick(b_tile, ROUNDS[1], y, moved)

    part = [f[3 * SB * q : 3 * SB * (q + 1)] for q in range(4)]
    got = [send(part[q], [(device(0, 0, 0, 0), device(0, 0, 0, q))]) for q in (1, 3, 2)]
    mine = jnp.where(x == 0, part[0], jnp.where(x == 1, got[0], jnp.where(x == 2, got[2], got[1])))

    def factor_y(a, b):
        return [(device(a, 0, 0, j), device(b, 0, 0, j)) for j in range(NX)]

    def factor_z(a, b):
        return [(device(i, 0, a, j), device(i, 0, b, j)) for i in range(NY) for j in range(NX)]

    def shift_x(by, cores):
        return [
            (device(i, c, k, j), device(i, c, k, (j + by) % NX))
            for i in range(NY)
            for c in cores
            for k in range(NZ)
            for j in range(NX)
        ]

    across = [(device(i, 0, k, j), device(i, 1, k, j)) for i in range(NY) for k in range(NZ) for j in range(NX)]

    got = ring_sends(own, ROUNDS[1], along_z)
    mine = ring_round(mine, ROUNDS[0], y, factor_y)
    b_other = send(b_tile, across)
    mine, got, b_other = lax.optimization_barrier((mine, got, b_other))
    own = ring_pick(own, ROUNDS[1], z, got)
    b_tile = jnp.where(core == 1, b_other, b_tile)

    left = send(own, shift_x(1, (0, 1)))
    right = send(own, shift_x(-1, (0, 1)))
    mine = ring_round(mine, ROUNDS[1], y, factor_y)
    mine = ring_round(mine, ROUNDS[0], z, factor_z)
    mine, left, right = lax.optimization_barrier((mine, left, right))

    opp_a = send(left[: HB // 2], shift_x(1, (0, 1)))
    opp_b = send(right[HB // 2 :], shift_x(-1, (0, 1)))
    mine = ring_round(mine, ROUNDS[1], z, factor_z)
    turned = jnp.concatenate([mine] + [send(mine, shift_x(-by, (0,))) for by in (1, 2, 3)], axis=0)
    turned = jnp.where(core == 1, send(turned, across), turned)

    pos = jnp.stack([row, col, x, 0]).astype(jnp.int32)
    out = update(pos, own, left, right, opp_a, opp_b, b_tile, turned, w, cov)
    return out.reshape(covariance.shape)


def solution(mesh):
    return jax.shard_map(
        on_device,
        mesh=mesh,
        in_specs=(P(None, "row", None, "col"),),
        out_specs=P(None, "row", None, "col"),
        check_vma=False,
    )
```

```python
import jax
import jax.numpy as jnp
from jax import lax
from jax.experimental import pallas as pl
from jax.experimental.pallas import tpu as pltpu
from jax.sharding import PartitionSpec as P

AXES = ("row", "col")
ROWS, COLS = 16, 32
NZ, NX = 8, 4
TB = 512
SB = 128
HB = 256
SLOTS = 12
HIGHEST = lax.Precision.HIGHEST
M0, M1, X10, L20, L21, L30, L31, M2, M3, X32 = range(10)


def nn(a, b):
    return lax.dot_general(a, b, (((1,), (0,)), ((), ())), precision=HIGHEST, preferred_element_type=jnp.float32)


def nt(a, b):
    return lax.dot_general(a, b, (((1,), (1,)), ((), ())), precision=HIGHEST, preferred_element_type=jnp.float32)


def factor_block(block):
    tiles = SB // 8
    lane = lax.broadcasted_iota(jnp.int32, (8, SB), 1)
    sub = lax.broadcasted_iota(jnp.int32, (8, SB), 0)
    s = [block[8 * t : 8 * t + 8, :] for t in range(tiles)]
    e = [jnp.where(lane == sub + 8 * t, 1.0, 0.0).astype(jnp.float32) for t in range(tiles)]
    upper, inverse = [], []
    for b in range(tiles):
        cols = [
            [jnp.broadcast_to(s[t][:, 8 * b + m : 8 * b + m + 1], (8, SB)) for t in range(b, tiles)]
            for m in range(8)
        ]
        top, top_e = s[b], e[b]
        out_u, out_e = jnp.zeros_like(top), jnp.zeros_like(top)
        done = []
        for m in range(8):
            d = jnp.broadcast_to(cols[m][0][m : m + 1, :], (8, SB))
            r = lax.rsqrt(d)
            r = r * (1.5 - (0.5 * d) * (r * r))
            lc = [c * r for c in cols[m]]
            ur = jnp.broadcast_to(top[m : m + 1, :], (8, SB)) * r
            er = jnp.broadcast_to(top_e[m : m + 1, :], (8, SB)) * r
            out_u = jnp.where(sub == m, ur, out_u)
            out_e = jnp.where(sub == m, er, out_e)
            for k in range(m + 1, 8):
                f = jnp.broadcast_to(lc[0][k : k + 1, :], (8, SB))
                cols[k] = [c - l * f for c, l in zip(cols[k], lc)]
            below = jnp.where(sub > m, lc[0], 0.0)
            top = top - below * ur
            top_e = top_e - below * er
            done.append((lc, ur, er))
        for t in range(b + 1, tiles):
            for lc, ur, er in done:
                s[t] = s[t] - lc[t - b] * ur
                e[t] = e[t] - lc[t - b] * er
        upper.append(jnp.where(lane >= sub + 8 * b, out_u, 0.0))
        inverse.append(out_e)
    return jnp.concatenate(upper, axis=0), jnp.concatenate(inverse, axis=0)


def wide(ref, first, rows, lo=0, hi=4):
    return jnp.concatenate([ref[pl.ds(4 * first + i, rows, stride=4), :] for i in range(lo, hi)], axis=1)


def put_wide(ref, first, value):
    for i in range(value.shape[1] // SB):
        ref[pl.ds(4 * first + i, value.shape[0], stride=4), :] = value[:, i * SB : (i + 1) * SB]


def factor_kernel(flag_ref, a_ref, low_ref, f_ref, w_ref):
    @pl.when(flag_ref[0] == 1)
    def _():
        def slot(i):
            return pl.ds(i * SB, SB)

        w_ref[...] = wide(a_ref, 0, TB)
        for k in range(4):
            lo, hi = k * SB, (k + 1) * SB
            u, inv = factor_block(w_ref[lo:hi, lo:hi])
            f_ref[slot((M0, M1, M2, M3)[k]), :] = inv
            w_ref[lo:hi, lo:hi] = u.T
            if hi < TB:
                below = nt(w_ref[hi:, lo:hi], inv)
                w_ref[hi:, hi:] = w_ref[hi:, hi:] - nt(below, below)
                w_ref[hi:, lo:hi] = below
                w_ref[lo:hi, hi:] = jnp.zeros((SB, TB - hi), jnp.float32)
                if k < 2:
                    f_ref[slot((L20, L21)[k]), :] = below[2 * SB - hi : 3 * SB - hi]
                    f_ref[slot((L30, L31)[k]), :] = below[3 * SB - hi : 4 * SB - hi]
            if k % 2 == 1:
                prev = f_ref[slot((M0, M2)[k // 2]), :]
                f_ref[slot((X10, X32)[k // 2]), :] = -nn(inv, nn(w_ref[lo:hi, lo - SB : lo], prev))
        put_wide(low_ref, 0, w_ref[...])


def factor_tile(flag, a):
    vmem = pl.BlockSpec(memory_space=pltpu.VMEM)
    return pl.pallas_call(
        factor_kernel,
        out_shape=(
            jax.ShapeDtypeStruct((4 * TB, SB), jnp.float32),
            jax.ShapeDtypeStruct((SLOTS * SB, SB), jnp.float32),
        ),
        in_specs=[pl.BlockSpec(memory_space=pltpu.SMEM), vmem],
        out_specs=(vmem, vmem),
        scratch_shapes=[pltpu.VMEM((TB, TB), jnp.float32)],
        cost_estimate=pl.CostEstimate(flops=20_000_000_000, bytes_accessed=3_000_000, transcendentals=0),
        compiler_params=pltpu.CompilerParams(vmem_limit_bytes=24 * 1024 * 1024),
        name="factor",
    )(flag, a)


def update_kernel(pos_ref, own_ref, left_ref, right_ref, opp_a_ref, opp_b_ref, b_ref, f_ref, low_ref, cov_ref, out_ref, y_ref):
    row, col, x = pos_ref[0], pos_ref[1], pos_ref[2]

    def block(i):
        place = lax.rem(i // 3 - x + 4, 4)
        return f_ref[pl.ds(pl.multiple_of(place * (3 * SB) + (i % 3) * SB, SB), SB), :]

    zero = jnp.zeros((SB, SB), jnp.float32)

    def square(a, b, c, d):
        return jnp.concatenate(
            [jnp.concatenate([a, b], axis=1), jnp.concatenate([c, d], axis=1)], axis=0
        )

    d0 = square(block(M0), zero, block(X10), block(M1))
    d1 = square(block(M2), zero, block(X32), block(M3))
    g = square(block(L20), block(L21), block(L30), block(L31))
    y0 = nn(d0, wide(b_ref, 0, HB))
    y_ref[0:HB, :] = y0
    y_ref[HB:TB, :] = nn(d1, wide(b_ref, HB, HB) - nn(g, y0))

    def piece(q, raw0, raw1):
        x0 = nt(raw0, d0)
        x1 = nt(raw1 - nt(x0, g), d1)
        xs = jnp.concatenate([x0, x1], axis=1)
        tile_row = row + ROWS * (q // 2)

        @pl.when(col > 0)
        def _():
            cov = wide(cov_ref, q * HB, HB)
            new = cov - nn(xs, y_ref[...])
            put_wide(out_ref, q * HB, jnp.where(tile_row >= col, new, cov))

        @pl.when(col == 0)
        def _():
            low = wide(low_ref, lax.rem(q, 2) * HB, HB)
            put_wide(out_ref, q * HB, jnp.where(tile_row == 0, low, xs))

    for shift, ref in ((0, own_ref), (3, left_ref), (1, right_ref)):
        piece(lax.rem(x + shift, 4), wide(ref, 0, HB, 0, 2), wide(ref, 0, HB, 2, 4))
    half = HB // 2
    opp0 = jnp.concatenate([wide(opp_a_ref, 0, half, 0, 2), wide(opp_b_ref, 0, half, 0, 2)], axis=0)
    opp1 = jnp.concatenate([wide(opp_a_ref, 0, half, 2, 4), wide(opp_b_ref, 0, half, 2, 4)], axis=0)
    piece(lax.rem(x + 2, 4), opp0, opp1)


def update(pos, own, left, right, opp_a, opp_b, b, f, low, cov):
    vmem = pl.BlockSpec(memory_space=pltpu.VMEM)
    return pl.pallas_call(
        update_kernel,
        out_shape=jax.ShapeDtypeStruct((8 * TB, SB), jnp.float32),
        in_specs=[pl.BlockSpec(memory_space=pltpu.SMEM)] + [vmem] * 9,
        out_specs=vmem,
        scratch_shapes=[pltpu.VMEM((TB, TB), jnp.float32)],
        cost_estimate=pl.CostEstimate(flops=8_000_000_000, bytes_accessed=9_000_000, transcendentals=0),
        compiler_params=pltpu.CompilerParams(vmem_limit_bytes=40 * 1024 * 1024),
        name="update",
    )(pos, own, left, right, opp_a, opp_b, b, f, low, cov)


def send(value, pairs):
    return lax.ppermute(value, AXES, pairs)


def one_of(pos, places):
    found = pos == places[0]
    for place in places[1:]:
        found = jnp.logical_or(found, pos == place)
    return found


ROUNDS = (
    (((0, 3),), ((0, 5),)),
    (((0, 1), (3, 4), (5, 6)), ((0, 7), (3, 2))),
)


def ring_sends(value, moves, lift):
    return [send(value, [p for a, b in pairs for p in lift(a, b)]) for pairs in moves]


def ring_pick(value, moves, pos, got):
    for pairs, received in zip(moves, got):
        value = jnp.where(one_of(pos, [b for _, b in pairs]), received, value)
    return value


def ring_round(value, moves, pos, lift):
    return ring_pick(value, moves, pos, ring_sends(value, moves, lift))


def last_col(row, quarter):
    return row if quarter < 2 else row + ROWS


CHILDREN = {0: (3, 5, 1, 7), 3: (2, 4), 5: (6,), 1: (), 2: (), 4: (), 6: (), 7: ()}


def reaches(place, last):
    return NX * place <= last or any(reaches(c, last) for c in CHILDREN[place])


def on_device(covariance):
    row = lax.axis_index("row")
    col = lax.axis_index("col")
    y, core = row // 2, row % 2
    z, x = col // NX, col % NX
    cov = covariance.reshape(8 * TB, SB)
    is_root = jnp.logical_and(row == 0, col == 0)
    flag = is_root.astype(jnp.int32).reshape(1)
    rows = range(ROWS)
    quarter_rows = HB * 4

    def at(i, k, j):
        return i * COLS + k * NX + j

    def tied(*values):
        return lax.optimization_barrier(values)

    def scatter(q):
        return [(at(i, 0, 0), at(i, 0, q)) for i in rows if last_col(i, q) > 0]

    def along_z(a, b):
        return [(at(i, a, j), at(i, b, j)) for i in rows for j in range(NX) if last_col(i, j) > 0 and reaches(b, last_col(i, j))]

    def shift_x(by, cores):
        return [
            (at(i, k, j), at(i, k, (j + by) % NX))
            for i in rows
            if i % 2 in cores
            for k in range(NZ)
            for j in range(NX)
            if len(cores) == 1 or NX * k <= last_col(i, 2)
        ]

    def along_y(a, b):
        return [(at(2 * a, k, j), at(2 * b, k, j)) for k in range(NZ) for j in range(NX) if k + j > 0]

    across = [(at(i, k, j), at(i + 1, k, j)) for i in rows[::2] for k in range(NZ) for j in range(NX)]

    def factor_y(a, b):
        return [(at(2 * a, 0, j), at(2 * b, 0, j)) for j in range(NX)]

    def factor_z(a, b):
        return [(at(i, a, j), at(i, b, j)) for i in rows[::2] for j in range(NX)]

    def by_x(values):
        return jnp.where(x == 0, values[0], jnp.where(x == 1, values[1], jnp.where(x == 2, values[2], values[3])))

    quarter = [cov[quarter_rows * q : quarter_rows * (q + 1)] for q in range(4)]
    got = [send(quarter[q], scatter(q)) for q in (3, 2, 1)]
    low, f = factor_tile(flag, cov[0 : 4 * TB])

    got, f, b_tile = tied(got, f, cov[0 : 4 * TB])
    own = by_x([quarter[0], got[2], got[1], got[0]])
    moved = ring_sends(b_tile, ROUNDS[0], along_y)
    got = ring_sends(own, ROUNDS[0], along_z)

    f, got, moved = tied(f, got, moved)
    own = ring_pick(own, ROUNDS[0], z, got)
    b_tile = ring_pick(b_tile, ROUNDS[0], y, moved)
    got = ring_sends(own, ROUNDS[1], along_z)
    moved = ring_sends(b_tile, ROUNDS[1], along_y)

    part = [f[3 * SB * q : 3 * SB * (q + 1)] for q in range(4)]
    given = [send(part[q], [(0, q)]) for q in (1, 2, 3)]
    mine = by_x([part[0]] + given)

    mine, got, moved = tied(mine, got, moved)
    own = ring_pick(own, ROUNDS[1], z, got)
    b_tile = ring_pick(b_tile, ROUNDS[1], y, moved)
    left = send(own, shift_x(1, (0, 1)))
    right = send(own, shift_x(-1, (0, 1)))
    mine = ring_round(mine, ROUNDS[0], y, factor_y)
    mine, b_tile = tied(mine, b_tile)
    b_other = send(b_tile, across)
    mine = ring_round(mine, ROUNDS[1], y, factor_y)
    mine = ring_round(mine, ROUNDS[0], z, factor_z)

    mine, left, right, b_other = tied(mine, left, right, b_other)
    b_tile = jnp.where(core == 1, b_other, b_tile)
    opp_a = send(left[: quarter_rows // 2], shift_x(1, (0, 1)))
    opp_b = send(right[quarter_rows // 2 :], shift_x(-1, (0, 1)))
    mine = ring_round(mine, ROUNDS[1], z, factor_z)

    mine, opp_a, opp_b, b_tile = tied(mine, opp_a, opp_b, b_tile)
    turned = jnp.concatenate([mine] + [send(mine, shift_x(-by, (0,))) for by in (1, 2, 3)], axis=0)
    turned = jnp.where(core == 1, send(turned, across), turned)

    pos = jnp.stack([row, col, x, 0]).astype(jnp.int32)
    out = update(pos, own, left, right, opp_a, opp_b, b_tile, turned, low, cov)
    return out.reshape(covariance.shape)


def solution(mesh):
    return jax.shard_map(
        on_device,
        mesh=mesh,
        in_specs=(P(None, "row", None, "col"),),
        out_specs=P(None, "row", None, "col"),
        check_vma=False,
    )
```

```python
import jax
import jax.numpy as jnp
from jax import lax
from jax.experimental import pallas as pl
from jax.experimental.pallas import tpu as pltpu
from jax.sharding import PartitionSpec as P

AXES = ("row", "col")
ROWS, COLS = 16, 32
NZ, NX = 8, 4
HOME_ROW, HOME_Z = 1, 7
TB = 512
SB = 128
HB = 256
SLOTS = 12
HIGHEST = lax.Precision.HIGHEST
M0, M1, X10, L20, L21, L30, L31, M2, M3, X32 = range(10)


def nn(a, b):
    return lax.dot_general(a, b, (((1,), (0,)), ((), ())), precision=HIGHEST, preferred_element_type=jnp.float32)


def nt(a, b):
    return lax.dot_general(a, b, (((1,), (1,)), ((), ())), precision=HIGHEST, preferred_element_type=jnp.float32)


def factor_block(block):
    tiles = SB // 8
    lane = lax.broadcasted_iota(jnp.int32, (8, SB), 1)
    sub = lax.broadcasted_iota(jnp.int32, (8, SB), 0)
    s = [block[8 * t : 8 * t + 8, :] for t in range(tiles)]
    e = [jnp.where(lane == sub + 8 * t, 1.0, 0.0).astype(jnp.float32) for t in range(tiles)]
    inverse = []
    for b in range(tiles):
        cols = [
            [jnp.broadcast_to(s[t][:, 8 * b + m : 8 * b + m + 1], (8, SB)) for t in range(b, tiles)]
            for m in range(8)
        ]
        top, top_e = s[b], e[b]
        out_e = jnp.zeros_like(top)
        done = []
        for m in range(8):
            d = jnp.broadcast_to(cols[m][0][m : m + 1, :], (8, SB))
            r = lax.rsqrt(d)
            r = r * (1.5 - (0.5 * d) * (r * r))
            lc = [c * r for c in cols[m]]
            ur = jnp.broadcast_to(top[m : m + 1, :], (8, SB)) * r
            er = jnp.broadcast_to(top_e[m : m + 1, :], (8, SB)) * r
            out_e = jnp.where(sub == m, er, out_e)
            for k in range(m + 1, 8):
                f = jnp.broadcast_to(lc[0][k : k + 1, :], (8, SB))
                cols[k] = [c - l * f for c, l in zip(cols[k], lc)]
            below = jnp.where(sub > m, lc[0], 0.0)
            top = top - below * ur
            top_e = top_e - below * er
            done.append((lc, ur, er))
        for t in range(b + 1, tiles):
            for lc, ur, er in done:
                s[t] = s[t] - lc[t - b] * ur
                e[t] = e[t] - lc[t - b] * er
        inverse.append(out_e)
    return jnp.concatenate(inverse, axis=0)


def wide(ref, first, rows, lo=0, hi=4):
    return jnp.concatenate([ref[pl.ds(4 * first + i, rows, stride=4), :] for i in range(lo, hi)], axis=1)


def put_wide(ref, first, value):
    for i in range(value.shape[1] // SB):
        ref[pl.ds(4 * first + i, value.shape[0], stride=4), :] = value[:, i * SB : (i + 1) * SB]


def factor_kernel(flag_ref, a_ref, f_ref, w_ref):
    @pl.when(flag_ref[0] == 1)
    def _():
        def slot(i):
            return pl.ds(i * SB, SB)

        w_ref[...] = wide(a_ref, 0, TB)
        for k in range(4):
            lo, hi = k * SB, (k + 1) * SB
            inv = factor_block(w_ref[lo:hi, lo:hi])
            f_ref[slot((M0, M1, M2, M3)[k]), :] = inv
            if hi < TB:
                below = nt(w_ref[hi:, lo:hi], inv)
                w_ref[hi:, hi:] = w_ref[hi:, hi:] - nt(below, below)
                w_ref[hi:, lo:hi] = below
                if k < 2:
                    f_ref[slot((L20, L21)[k]), :] = below[2 * SB - hi : 3 * SB - hi]
                    f_ref[slot((L30, L31)[k]), :] = below[3 * SB - hi : 4 * SB - hi]
            if k % 2 == 1:
                prev = f_ref[slot((M0, M2)[k // 2]), :]
                f_ref[slot((X10, X32)[k // 2]), :] = -nn(inv, nn(w_ref[lo:hi, lo - SB : lo], prev))


def factor_tile(flag, a):
    vmem = pl.BlockSpec(memory_space=pltpu.VMEM)
    return pl.pallas_call(
        factor_kernel,
        out_shape=jax.ShapeDtypeStruct((SLOTS * SB, SB), jnp.float32),
        in_specs=[pl.BlockSpec(memory_space=pltpu.SMEM), vmem],
        out_specs=vmem,
        scratch_shapes=[pltpu.VMEM((TB, TB), jnp.float32)],
        cost_estimate=pl.CostEstimate(flops=20_000_000_000, bytes_accessed=3_000_000, transcendentals=0),
        compiler_params=pltpu.CompilerParams(vmem_limit_bytes=24 * 1024 * 1024),
        name="factor",
    )(flag, a)


def update_kernel(pos_ref, own_ref, left_ref, right_ref, opp_a_ref, opp_b_ref, b_ref, f_ref, cov_ref, out_ref, y_ref):
    row, col, x = pos_ref[0], pos_ref[1], pos_ref[2]

    def block(i):
        place = lax.rem(i // 3 - x + 4, 4)
        return f_ref[pl.ds(pl.multiple_of(place * (3 * SB) + (i % 3) * SB, SB), SB), :]

    zero = jnp.zeros((SB, SB), jnp.float32)

    def square(a, b, c, d):
        return jnp.concatenate(
            [jnp.concatenate([a, b], axis=1), jnp.concatenate([c, d], axis=1)], axis=0
        )

    d0 = square(block(M0), zero, block(X10), block(M1))
    d1 = square(block(M2), zero, block(X32), block(M3))
    g = square(block(L20), block(L21), block(L30), block(L31))
    y0 = nn(d0, wide(b_ref, 0, HB))
    y_ref[0:HB, :] = y0
    y_ref[HB:TB, :] = nn(d1, wide(b_ref, HB, HB) - nn(g, y0))

    def piece(q, raw0, raw1):
        x0 = nt(raw0, d0)
        x1 = nt(raw1 - nt(x0, g), d1)
        xs = jnp.concatenate([x0, x1], axis=1)
        tile_row = row + ROWS * (q // 2)

        @pl.when(col > 0)
        def _():
            cov = wide(cov_ref, q * HB, HB)
            new = cov - nn(xs, y_ref[...])
            put_wide(out_ref, q * HB, jnp.where(tile_row >= col, new, cov))

        @pl.when(col == 0)
        def _():
            at_row = lax.rem(q, 2) * HB + lax.broadcasted_iota(jnp.int32, (HB, TB), 0)
            above = lax.broadcasted_iota(jnp.int32, (HB, TB), 1) > at_row
            put_wide(out_ref, q * HB, jnp.where(jnp.logical_and(tile_row == 0, above), 0.0, xs))

    for shift, ref in ((0, own_ref), (3, left_ref), (1, right_ref)):
        piece(lax.rem(x + shift, 4), wide(ref, 0, HB, 0, 2), wide(ref, 0, HB, 2, 4))
    half = HB // 2
    opp0 = jnp.concatenate([wide(opp_a_ref, 0, half, 0, 2), wide(opp_b_ref, 0, half, 0, 2)], axis=0)
    opp1 = jnp.concatenate([wide(opp_a_ref, 0, half, 2, 4), wide(opp_b_ref, 0, half, 2, 4)], axis=0)
    piece(lax.rem(x + 2, 4), opp0, opp1)


def update(pos, own, left, right, opp_a, opp_b, b, f, cov):
    vmem = pl.BlockSpec(memory_space=pltpu.VMEM)
    return pl.pallas_call(
        update_kernel,
        out_shape=jax.ShapeDtypeStruct((8 * TB, SB), jnp.float32),
        in_specs=[pl.BlockSpec(memory_space=pltpu.SMEM)] + [vmem] * 8,
        out_specs=vmem,
        scratch_shapes=[pltpu.VMEM((TB, TB), jnp.float32)],
        cost_estimate=pl.CostEstimate(flops=8_000_000_000, bytes_accessed=9_000_000, transcendentals=0),
        compiler_params=pltpu.CompilerParams(vmem_limit_bytes=40 * 1024 * 1024),
        name="update",
    )(pos, own, left, right, opp_a, opp_b, b, f, cov)


def send(value, pairs):
    return lax.ppermute(value, AXES, pairs)


def one_of(pos, places):
    found = pos == places[0]
    for place in places[1:]:
        found = jnp.logical_or(found, pos == place)
    return found


ROUNDS = (
    (((0, 3),), ((0, 5),)),
    (((0, 1), (3, 4), (5, 6)), ((0, 7), (3, 2))),
)


def ring_sends(value, moves, lift):
    return [send(value, [p for a, b in pairs for p in lift(a, b)]) for pairs in moves]


def ring_pick(value, moves, pos, got):
    for pairs, received in zip(moves, got):
        value = jnp.where(one_of(pos, [b for _, b in pairs]), received, value)
    return value


def ring_round(value, moves, pos, lift):
    return ring_pick(value, moves, pos, ring_sends(value, moves, lift))


def last_col(row, quarter):
    return row if quarter < 2 else row + ROWS


CHILDREN = {0: (3, 5, 1, 7), 3: (2, 4), 5: (6,), 1: (), 2: (), 4: (), 6: (), 7: ()}


def reaches(place, last):
    return NX * place <= last or any(reaches(c, last) for c in CHILDREN[place])


def on_device(covariance):
    row = lax.axis_index("row")
    col = lax.axis_index("col")
    y, core = row // 2, row % 2
    z, x = col // NX, col % NX
    cov = covariance.reshape(8 * TB, SB)
    flag = jnp.logical_and(row == HOME_ROW, col == HOME_Z * NX).astype(jnp.int32).reshape(1)
    rows = range(ROWS)
    quarter_rows = HB * 4

    def at(i, k, j):
        return i * COLS + k * NX + j

    def tied(*values):
        return lax.optimization_barrier(values)

    def scatter(q):
        return [(at(i, 0, 0), at(i, 0, q)) for i in rows]

    def along_z(a, b):
        return [(at(i, a, j), at(i, b, j)) for i in rows for j in range(NX) if last_col(i, j) > 0 and reaches(b, last_col(i, j))]

    def shift_x(by, cores):
        return [
            (at(i, k, j), at(i, k, (j + by) % NX))
            for i in rows
            if i % 2 in cores
            for k in range(NZ)
            for j in range(NX)
            if len(cores) == 1 or NX * k <= last_col(i, 2)
        ]

    def along_y(a, b):
        return [(at(2 * a, k, j), at(2 * b, k, j)) for k in range(NZ) for j in range(NX) if k + j > 0]

    across = [(at(i, k, j), at(i + 1, k, j)) for i in rows[::2] for k in range(NZ) for j in range(NX)]

    def factor_y(a, b):
        return [(at(2 * a + 1, HOME_Z, j), at(2 * b + 1, HOME_Z, j)) for j in range(NX)]

    def factor_z(a, b):
        return [(at(i, (a + HOME_Z) % NZ, j), at(i, (b + HOME_Z) % NZ, j)) for i in rows[1::2] for j in range(NX)]

    home = at(HOME_ROW, HOME_Z, 0)
    home_z = (z - HOME_Z + NZ) % NZ

    def by_x(values):
        return jnp.where(x == 0, values[0], jnp.where(x == 1, values[1], jnp.where(x == 2, values[2], values[3])))

    b_tile = cov[0 : 4 * TB]
    corner = send(b_tile, [(0, home)])
    quarter = [cov[quarter_rows * q : quarter_rows * (q + 1)] for q in range(4)]
    got = [send(quarter[q], scatter(q)) for q in (3, 2, 1)]
    moved = ring_sends(b_tile, ROUNDS[0], along_y)
    corner, got = tied(corner, got)
    own = by_x([quarter[0], got[2], got[1], got[0]])
    got = ring_sends(own, ROUNDS[0], along_z)

    corner, got, moved = tied(corner, got, moved)
    own = ring_pick(own, ROUNDS[0], z, got)
    got = ring_sends(own, ROUNDS[1], along_z)
    b_tile = ring_pick(b_tile, ROUNDS[0], y, moved)
    moved = ring_sends(b_tile, ROUNDS[1], along_y)
    f = factor_tile(flag, corner)

    part = [f[3 * SB * q : 3 * SB * (q + 1)] for q in range(4)]
    mine = by_x([part[0]] + [send(part[q], [(home, home + q)]) for q in (1, 2, 3)])
    mine = ring_round(mine, ROUNDS[0], y, factor_y)
    mine = ring_round(mine, ROUNDS[1], y, factor_y)

    mine, got = tied(mine, got)
    own = ring_pick(own, ROUNDS[1], z, got)
    left = send(own, shift_x(1, (0, 1)))
    right = send(own, shift_x(-1, (0, 1)))
    mine = ring_round(mine, ROUNDS[0], home_z, factor_z)

    mine, left, right, moved = tied(mine, left, right, moved)
    b_tile = ring_pick(b_tile, ROUNDS[1], y, moved)
    opp_a = send(left[: quarter_rows // 2], shift_x(1, (0, 1)))
    opp_b = send(right[quarter_rows // 2 :], shift_x(-1, (0, 1)))
    b_other = send(b_tile, across)
    mine = ring_round(mine, ROUNDS[1], home_z, factor_z)

    mine, opp_a, opp_b, b_other = tied(mine, opp_a, opp_b, b_other)
    b_tile = jnp.where(core == 1, b_other, b_tile)
    turned = jnp.concatenate([mine] + [send(mine, shift_x(-by, (1,))) for by in (1, 2, 3)], axis=0)
    turned = jnp.where(core == 0, send(turned, [(b, a) for a, b in across]), turned)

    pos = jnp.stack([row, col, x, 0]).astype(jnp.int32)
    out = update(pos, own, left, right, opp_a, opp_b, b_tile, turned, cov)
    return out.reshape(covariance.shape)


def solution(mesh):
    return jax.shard_map(
        on_device,
        mesh=mesh,
        in_specs=(P(None, "row", None, "col"),),
        out_specs=P(None, "row", None, "col"),
        check_vma=False,
    )
```

```python
import jax
import jax.numpy as jnp
from jax import lax
from jax.experimental import pallas as pl
from jax.experimental.pallas import tpu as pltpu
from jax.sharding import PartitionSpec as P

AXES = ("row", "col")
ROWS, COLS = 16, 32
NZ, NX = 8, 4
HOME_ROW, HOME_Z = 1, 7
TB = 512
SB = 128
HB = 256
SLOTS = 12
HIGHEST = lax.Precision.HIGHEST
M0, M1, X10, L20, L21, L30, L31, M2, M3, X32 = range(10)


def nn(a, b):
    return lax.dot_general(a, b, (((1,), (0,)), ((), ())), precision=HIGHEST, preferred_element_type=jnp.float32)


def nt(a, b):
    return lax.dot_general(a, b, (((1,), (1,)), ((), ())), precision=HIGHEST, preferred_element_type=jnp.float32)


def factor_block(block):
    tiles = SB // 8
    lane = lax.broadcasted_iota(jnp.int32, (8, SB), 1)
    sub = lax.broadcasted_iota(jnp.int32, (8, SB), 0)
    s = [block[8 * t : 8 * t + 8, :] for t in range(tiles)]
    e = [jnp.where(lane == sub + 8 * t, 1.0, 0.0).astype(jnp.float32) for t in range(tiles)]
    inverse = []
    for b in range(tiles):
        cols = [
            [jnp.broadcast_to(s[t][:, 8 * b + m : 8 * b + m + 1], (8, SB)) for t in range(b, tiles)]
            for m in range(8)
        ]
        top, top_e = s[b], e[b]
        out_e = jnp.zeros_like(top)
        done = []
        for m in range(8):
            d = jnp.broadcast_to(cols[m][0][m : m + 1, :], (8, SB))
            r = lax.rsqrt(d)
            r = r * (1.5 - (0.5 * d) * (r * r))
            lc = [c * r for c in cols[m]]
            ur = jnp.broadcast_to(top[m : m + 1, :], (8, SB)) * r
            er = jnp.broadcast_to(top_e[m : m + 1, :], (8, SB)) * r
            out_e = jnp.where(sub == m, er, out_e)
            for k in range(m + 1, 8):
                f = jnp.broadcast_to(lc[0][k : k + 1, :], (8, SB))
                cols[k] = [c - l * f for c, l in zip(cols[k], lc)]
            below = jnp.where(sub > m, lc[0], 0.0)
            top = top - below * ur
            top_e = top_e - below * er
            done.append((lc, ur, er))
        for t in range(b + 1, tiles):
            for lc, ur, er in done:
                s[t] = s[t] - lc[t - b] * ur
                e[t] = e[t] - lc[t - b] * er
        inverse.append(out_e)
    return jnp.concatenate(inverse, axis=0)


def wide(ref, first, rows, lo=0, hi=4):
    return jnp.concatenate([ref[pl.ds(4 * first + i, rows, stride=4), :] for i in range(lo, hi)], axis=1)


def put_wide(ref, first, value):
    for i in range(value.shape[1] // SB):
        ref[pl.ds(4 * first + i, value.shape[0], stride=4), :] = value[:, i * SB : (i + 1) * SB]


def factor_kernel(flag_ref, a_ref, f_ref, w_ref):
    @pl.when(flag_ref[0] == 1)
    def _():
        def slot(i):
            return pl.ds(i * SB, SB)

        w_ref[...] = wide(a_ref, 0, TB)
        for k in range(4):
            lo, hi = k * SB, (k + 1) * SB
            inv = factor_block(w_ref[lo:hi, lo:hi])
            f_ref[slot((M0, M1, M2, M3)[k]), :] = inv
            if hi < TB:
                below = nt(w_ref[hi:, lo:hi], inv)
                w_ref[hi:, hi:] = w_ref[hi:, hi:] - nt(below, below)
                w_ref[hi:, lo:hi] = below
                if k < 2:
                    f_ref[slot((L20, L21)[k]), :] = below[2 * SB - hi : 3 * SB - hi]
                    f_ref[slot((L30, L31)[k]), :] = below[3 * SB - hi : 4 * SB - hi]
            if k % 2 == 1:
                prev = f_ref[slot((M0, M2)[k // 2]), :]
                f_ref[slot((X10, X32)[k // 2]), :] = -nn(inv, nn(w_ref[lo:hi, lo - SB : lo], prev))


def factor_tile(flag, a):
    vmem = pl.BlockSpec(memory_space=pltpu.VMEM)
    return pl.pallas_call(
        factor_kernel,
        out_shape=jax.ShapeDtypeStruct((SLOTS * SB, SB), jnp.float32),
        in_specs=[pl.BlockSpec(memory_space=pltpu.SMEM), vmem],
        out_specs=vmem,
        scratch_shapes=[pltpu.VMEM((TB, TB), jnp.float32)],
        cost_estimate=pl.CostEstimate(flops=20_000_000_000, bytes_accessed=3_000_000, transcendentals=0),
        compiler_params=pltpu.CompilerParams(vmem_limit_bytes=24 * 1024 * 1024),
        name="factor",
    )(flag, a)


def update_kernel(pos_ref, own_ref, left_ref, right_ref, opp_ref, b_ref, b_other_ref, f0_ref, f3_ref, f1_ref, f2_ref, cov_ref, out_ref, y_ref, f_ref):
    row, col, x, core = pos_ref[0], pos_ref[1], pos_ref[2], pos_ref[3]
    part = 3 * SB
    for shift, ref in enumerate((f0_ref, f1_ref, f2_ref, f3_ref)):
        f_ref[pl.ds(pl.multiple_of(lax.rem(x + shift, 4) * part, SB), part), :] = ref[...]

    def block(i):
        return f_ref[i * SB : (i + 1) * SB, :]

    def b_rows(first):
        return jnp.where(core == 1, wide(b_other_ref, first, HB), wide(b_ref, first, HB))

    zero = jnp.zeros((SB, SB), jnp.float32)

    def square(a, b, c, d):
        return jnp.concatenate(
            [jnp.concatenate([a, b], axis=1), jnp.concatenate([c, d], axis=1)], axis=0
        )

    d0 = square(block(M0), zero, block(X10), block(M1))
    d1 = square(block(M2), zero, block(X32), block(M3))
    g = square(block(L20), block(L21), block(L30), block(L31))
    y0 = nn(d0, b_rows(0))
    y_ref[0:HB, :] = y0
    y_ref[HB:TB, :] = nn(d1, b_rows(HB) - nn(g, y0))

    def piece(q, raw0, raw1):
        x0 = nt(raw0, d0)
        x1 = nt(raw1 - nt(x0, g), d1)
        xs = jnp.concatenate([x0, x1], axis=1)
        tile_row = row + ROWS * (q // 2)

        @pl.when(col > 0)
        def _():
            cov = wide(cov_ref, q * HB, HB)
            new = cov - nn(xs, y_ref[...])
            put_wide(out_ref, q * HB, jnp.where(tile_row >= col, new, cov))

        @pl.when(col == 0)
        def _():
            at_row = lax.rem(q, 2) * HB + lax.broadcasted_iota(jnp.int32, (HB, TB), 0)
            above = lax.broadcasted_iota(jnp.int32, (HB, TB), 1) > at_row
            put_wide(out_ref, q * HB, jnp.where(jnp.logical_and(tile_row == 0, above), 0.0, xs))

    for shift, ref in ((0, own_ref), (3, left_ref), (1, right_ref), (2, opp_ref)):
        piece(lax.rem(x + shift, 4), wide(ref, 0, HB, 0, 2), wide(ref, 0, HB, 2, 4))


def update(*operands):
    vmem = pl.BlockSpec(memory_space=pltpu.VMEM)
    return pl.pallas_call(
        update_kernel,
        out_shape=jax.ShapeDtypeStruct((8 * TB, SB), jnp.float32),
        in_specs=[pl.BlockSpec(memory_space=pltpu.SMEM)] + [vmem] * (len(operands) - 1),
        out_specs=vmem,
        scratch_shapes=[pltpu.VMEM((TB, TB), jnp.float32), pltpu.VMEM((SLOTS * SB, SB), jnp.float32)],
        cost_estimate=pl.CostEstimate(flops=8_000_000_000, bytes_accessed=9_000_000, transcendentals=0),
        compiler_params=pltpu.CompilerParams(vmem_limit_bytes=40 * 1024 * 1024),
        name="update",
    )(*operands)


def send(value, pairs):
    return lax.ppermute(value, AXES, pairs)


def one_of(pos, places):
    found = pos == places[0]
    for place in places[1:]:
        found = jnp.logical_or(found, pos == place)
    return found


ROUNDS = (
    (((0, 3),), ((0, 5),)),
    (((0, 1), (3, 4), (5, 6)), ((0, 7), (3, 2))),
)


def ring_sends(value, moves, lift):
    return [send(value, [p for a, b in pairs for p in lift(a, b)]) for pairs in moves]


def ring_pick(value, moves, pos, got):
    for pairs, received in zip(moves, got):
        value = jnp.where(one_of(pos, [b for _, b in pairs]), received, value)
    return value


def ring_round(value, moves, pos, lift):
    return ring_pick(value, moves, pos, ring_sends(value, moves, lift))


def last_col(row, quarter):
    return row if quarter < 2 else row + ROWS


CHILDREN = {0: (3, 5, 1, 7), 3: (2, 4), 5: (6,), 1: (), 2: (), 4: (), 6: (), 7: ()}


def reaches(place, last):
    return NX * place <= last or any(reaches(c, last) for c in CHILDREN[place])


def on_device(covariance):
    row = lax.axis_index("row")
    col = lax.axis_index("col")
    y, core = row // 2, row % 2
    z, x = col // NX, col % NX
    cov = covariance.reshape(8 * TB, SB)
    flag = jnp.logical_and(row == HOME_ROW, col == HOME_Z * NX).astype(jnp.int32).reshape(1)
    rows = range(ROWS)
    quarter_rows = HB * 4

    def at(i, k, j):
        return i * COLS + k * NX + j

    def tied(*values):
        return lax.optimization_barrier(values)

    def scatter(q):
        return [(at(i, 0, 0), at(i, 0, q)) for i in rows]

    def along_z(a, b):
        return [(at(i, a, j), at(i, b, j)) for i in rows for j in range(NX) if last_col(i, j) > 0 and reaches(b, last_col(i, j))]

    def shift_x(by):
        return [(at(i, k, j), at(i, k, (j + by) % NX)) for i in rows for k in range(NZ) for j in range(NX)]

    def along_y(a, b):
        return [(at(2 * a, k, j), at(2 * b, k, j)) for k in range(NZ) for j in range(NX) if k + j > 0]

    across = [(at(i, k, j), at(i + 1, k, j)) for i in rows[::2] for k in range(NZ) for j in range(NX)]

    def factor_y(a, b):
        return [(at(2 * a + 1, HOME_Z, j), at(2 * b + 1, HOME_Z, j)) for j in range(NX)]

    def factor_z(a, b):
        return [(at(i, (a + HOME_Z) % NZ, j), at(i, (b + HOME_Z) % NZ, j)) for i in rows[1::2] for j in range(NX)]

    home = at(HOME_ROW, HOME_Z, 0)
    home_z = (z - HOME_Z + NZ) % NZ

    def by_x(values):
        return jnp.where(x == 0, values[0], jnp.where(x == 1, values[1], jnp.where(x == 2, values[2], values[3])))

    b_tile = cov[0 : 4 * TB]
    corner = send(b_tile, [(0, home)])
    quarter = [cov[quarter_rows * q : quarter_rows * (q + 1)] for q in range(4)]
    got = [send(quarter[q], scatter(q)) for q in (3, 2, 1)]
    moved = ring_sends(b_tile, ROUNDS[0], along_y)

    got, moved = tied(got, moved)
    own = by_x([quarter[0], got[2], got[1], got[0]])
    got = ring_sends(own, ROUNDS[0], along_z)
    b_tile = ring_pick(b_tile, ROUNDS[0], y, moved)
    moved = ring_sends(b_tile, ROUNDS[1], along_y)

    corner, got = tied(corner, got)
    f = factor_tile(flag, corner)
    f, got, moved = tied(f, got, moved)
    own = ring_pick(own, ROUNDS[0], z, got)
    got = ring_sends(own, ROUNDS[1], along_z)
    b_tile = ring_pick(b_tile, ROUNDS[1], y, moved)
    b_other = send(b_tile, across)

    part = [f[3 * SB * q : 3 * SB * (q + 1)] for q in range(4)]
    mine = by_x([part[0]] + [send(part[q], [(home, home + q)]) for q in (1, 2, 3)])
    mine = ring_round(mine, ROUNDS[0], y, factor_y)
    mine = ring_round(mine, ROUNDS[1], y, factor_y)

    mine, got = tied(mine, got)
    own = ring_pick(own, ROUNDS[1], z, got)
    left = send(own, shift_x(1))
    right = send(own, shift_x(-1))
    mine = ring_round(mine, ROUNDS[0], home_z, factor_z)

    mine, left, right = tied(mine, left, right)
    opposite = send(left, shift_x(1))
    mine = ring_round(mine, ROUNDS[1], home_z, factor_z)
    mine = jnp.where(core == 0, send(mine, [(b, a) for a, b in across]), mine)

    mine, opposite, b_other = tied(mine, opposite, b_other)
    f_left = send(mine, shift_x(1))
    f_right = send(mine, shift_x(-1))
    f_opposite = send(f_left, shift_x(1))

    pos = jnp.stack([row, col, x, core]).astype(jnp.int32)
    out = update(pos, own, left, right, opposite, b_tile, b_other, mine, f_left, f_right, f_opposite, cov)
    return out.reshape(covariance.shape)


def solution(mesh):
    return jax.shard_map(
        on_device,
        mesh=mesh,
        in_specs=(P(None, "row", None, "col"),),
        out_specs=P(None, "row", None, "col"),
        check_vma=False,
    )
```

```python
import jax
import jax.numpy as jnp
from jax import lax
from jax.experimental import pallas as pl
from jax.experimental.pallas import tpu as pltpu
from jax.sharding import PartitionSpec as P

AXES = ("row", "col")
ROWS, COLS = 16, 32
NZ, NX = 8, 4
HOME_ROW, HOME_Z = 1, 7
TB = 512
SB = 128
HB = 256
SLOTS = 12
HIGHEST = lax.Precision.HIGHEST
M0, M1, X10, L20, L21, L30, L31, M2, M3, X32 = range(10)


def nn(a, b):
    return lax.dot_general(a, b, (((1,), (0,)), ((), ())), precision=HIGHEST, preferred_element_type=jnp.float32)


def nt(a, b):
    return lax.dot_general(a, b, (((1,), (1,)), ((), ())), precision=HIGHEST, preferred_element_type=jnp.float32)


def factor_block(block):
    tiles = SB // 8
    lane = lax.broadcasted_iota(jnp.int32, (8, SB), 1)
    sub = lax.broadcasted_iota(jnp.int32, (8, SB), 0)
    s = [block[8 * t : 8 * t + 8, :] for t in range(tiles)]
    e = [jnp.where(lane == sub + 8 * t, 1.0, 0.0).astype(jnp.float32) for t in range(tiles)]
    inverse = []
    for b in range(tiles):
        cols = [
            [jnp.broadcast_to(s[t][:, 8 * b + m : 8 * b + m + 1], (8, SB)) for t in range(b, tiles)]
            for m in range(8)
        ]
        top, top_e = s[b], e[b]
        out_e = jnp.zeros_like(top)
        done = []
        for m in range(8):
            d = jnp.broadcast_to(cols[m][0][m : m + 1, :], (8, SB))
            r = lax.rsqrt(d)
            lc = [c * r for c in cols[m]]
            ur = jnp.broadcast_to(top[m : m + 1, :], (8, SB)) * r
            er = jnp.broadcast_to(top_e[m : m + 1, :], (8, SB)) * r
            out_e = jnp.where(sub == m, er, out_e)
            for k in range(m + 1, 8):
                f = jnp.broadcast_to(lc[0][k : k + 1, :], (8, SB))
                cols[k] = [c - l * f for c, l in zip(cols[k], lc)]
            below = jnp.where(sub > m, lc[0], 0.0)
            top = top - below * ur
            top_e = top_e - below * er
            done.append((lc, ur, er))
        for t in range(b + 1, tiles):
            for lc, ur, er in done:
                s[t] = s[t] - lc[t - b] * ur
                e[t] = e[t] - lc[t - b] * er
        inverse.append(out_e)
    return jnp.concatenate(inverse, axis=0)


def wide(ref, first, rows, lo=0, hi=4):
    return jnp.concatenate([ref[pl.ds(4 * first + i, rows, stride=4), :] for i in range(lo, hi)], axis=1)


def put_wide(ref, first, value):
    for i in range(value.shape[1] // SB):
        ref[pl.ds(4 * first + i, value.shape[0], stride=4), :] = value[:, i * SB : (i + 1) * SB]


def factor_kernel(flag_ref, a_ref, f_ref, w_ref):
    @pl.when(flag_ref[0] == 1)
    def _():
        def slot(i):
            return pl.ds(i * SB, SB)

        w_ref[...] = wide(a_ref, 0, TB)
        for k in range(4):
            lo, hi = k * SB, (k + 1) * SB
            inv = factor_block(w_ref[lo:hi, lo:hi])
            f_ref[slot((M0, M1, M2, M3)[k]), :] = inv
            if hi < TB:
                below = nt(w_ref[hi:, lo:hi], inv)
                w_ref[hi:, hi:] = w_ref[hi:, hi:] - nt(below, below)
                w_ref[hi:, lo:hi] = below
                if k < 2:
                    f_ref[slot((L20, L21)[k]), :] = below[2 * SB - hi : 3 * SB - hi]
                    f_ref[slot((L30, L31)[k]), :] = below[3 * SB - hi : 4 * SB - hi]
            if k % 2 == 1:
                prev = f_ref[slot((M0, M2)[k // 2]), :]
                f_ref[slot((X10, X32)[k // 2]), :] = -nn(inv, nn(w_ref[lo:hi, lo - SB : lo], prev))


def factor_tile(flag, a):
    vmem = pl.BlockSpec(memory_space=pltpu.VMEM)
    return pl.pallas_call(
        factor_kernel,
        out_shape=jax.ShapeDtypeStruct((SLOTS * SB, SB), jnp.float32),
        in_specs=[pl.BlockSpec(memory_space=pltpu.SMEM), vmem],
        out_specs=vmem,
        scratch_shapes=[pltpu.VMEM((TB, TB), jnp.float32)],
        cost_estimate=pl.CostEstimate(flops=20_000_000_000, bytes_accessed=3_000_000, transcendentals=0),
        compiler_params=pltpu.CompilerParams(vmem_limit_bytes=24 * 1024 * 1024),
        name="factor",
    )(flag, a)


def update_kernel(
    pos_ref, own_ref, left_ref, right_ref, opp_a_ref, opp_b_ref, b_ref, b_other_ref, f_ref, f_other_ref, cov_ref,
    out_ref, y_ref, raw_ref, x_ref,
):
    row, col, x, core = pos_ref[0], pos_ref[1], pos_ref[2], pos_ref[3]
    for shift, part, ref in ((0, 0, own_ref), (3, 0, left_ref), (1, 0, right_ref), (2, 0, opp_a_ref), (2, 1, opp_b_ref)):
        count = ref.shape[0] // 4
        first = lax.rem(x + shift, 4) * HB + part * count
        raw_ref[pl.ds(pl.multiple_of(first, SB), count), :] = wide(ref, 0, count)

    def block(i):
        place = lax.rem(i // 3 - x + 4, 4)
        rows = pl.ds(pl.multiple_of(place * (3 * SB) + (i % 3) * SB, SB), SB)
        return jnp.where(core == 0, f_other_ref[rows, :], f_ref[rows, :])

    def b_rows(first):
        return jnp.where(core == 1, wide(b_other_ref, first, HB), wide(b_ref, first, HB))

    zero = jnp.zeros((SB, SB), jnp.float32)

    def square(a, b, c, d):
        return jnp.concatenate(
            [jnp.concatenate([a, b], axis=1), jnp.concatenate([c, d], axis=1)], axis=0
        )

    d0 = square(block(M0), zero, block(X10), block(M1))
    d1 = square(block(M2), zero, block(X32), block(M3))
    g = square(block(L20), block(L21), block(L30), block(L31))
    x0 = nt(raw_ref[:, 0:HB], d0)
    x_ref[:, 0:HB] = x0
    x_ref[:, HB:TB] = nt(raw_ref[:, HB:TB] - nt(x0, g), d1)

    @pl.when(col > 0)
    def _():
        y0 = nn(d0, b_rows(0))
        y_ref[0:HB, :] = y0
        y_ref[HB:TB, :] = nn(d1, b_rows(HB) - nn(g, y0))
        prod = nn(x_ref[...], y_ref[...])
        for half in range(2):
            cov = wide(cov_ref, half * TB, TB)
            new = cov - prod[half * TB : (half + 1) * TB]
            put_wide(out_ref, half * TB, jnp.where(row + ROWS * half >= col, new, cov))

    @pl.when(col == 0)
    def _():
        above = lax.broadcasted_iota(jnp.int32, (TB, TB), 1) > lax.broadcasted_iota(jnp.int32, (TB, TB), 0)
        put_wide(out_ref, 0, jnp.where(jnp.logical_and(row == 0, above), 0.0, x_ref[0:TB, :]))
        put_wide(out_ref, TB, x_ref[TB:, :])


def update(*operands):
    vmem = pl.BlockSpec(memory_space=pltpu.VMEM)
    return pl.pallas_call(
        update_kernel,
        out_shape=jax.ShapeDtypeStruct((8 * TB, SB), jnp.float32),
        in_specs=[pl.BlockSpec(memory_space=pltpu.SMEM)] + [vmem] * (len(operands) - 1),
        out_specs=vmem,
        scratch_shapes=[pltpu.VMEM((rows, TB), jnp.float32) for rows in (TB, 2 * TB, 2 * TB)],
        cost_estimate=pl.CostEstimate(flops=8_000_000_000, bytes_accessed=9_000_000, transcendentals=0),
        compiler_params=pltpu.CompilerParams(vmem_limit_bytes=40 * 1024 * 1024),
        name="update",
    )(*operands)


def send(value, pairs):
    return lax.ppermute(value, AXES, pairs)


def one_of(pos, places):
    found = pos == places[0]
    for place in places[1:]:
        found = jnp.logical_or(found, pos == place)
    return found


ROUNDS = (
    (((0, 3),), ((0, 5),)),
    (((0, 1), (3, 4), (5, 6)), ((0, 7), (3, 2))),
)


FEWER = (
    (((0, 4),),),
    (((0, 1), (4, 5)), ((0, 7), (4, 3))),
    (((1, 2), (5, 6)),),
)


def ring_sends(value, moves, lift):
    return [send(value, [p for a, b in pairs for p in lift(a, b)]) for pairs in moves]


def ring_pick(value, moves, pos, got):
    for pairs, received in zip(moves, got):
        value = jnp.where(one_of(pos, [b for _, b in pairs]), received, value)
    return value


def ring_round(value, moves, pos, lift):
    return ring_pick(value, moves, pos, ring_sends(value, moves, lift))


def last_col(row, quarter):
    return row if quarter < 2 else row + ROWS


CHILDREN = {0: (3, 5, 1, 7), 3: (2, 4), 5: (6,), 1: (), 2: (), 4: (), 6: (), 7: ()}


def reaches(place, last):
    return NX * place <= last or any(reaches(c, last) for c in CHILDREN[place])


def on_device(covariance):
    row = lax.axis_index("row")
    col = lax.axis_index("col")
    y, core = row // 2, row % 2
    z, x = col // NX, col % NX
    cov = covariance.reshape(8 * TB, SB)
    flag = jnp.logical_and(row == HOME_ROW, col == HOME_Z * NX).astype(jnp.int32).reshape(1)
    rows = range(ROWS)
    quarter_rows = HB * 4

    def at(i, k, j):
        return i * COLS + k * NX + j

    def tied(*values):
        return lax.optimization_barrier(values)

    def scatter(q):
        return [(at(i, 0, 0), at(i, 0, q)) for i in rows]

    def along_z(a, b):
        return [(at(i, a, j), at(i, b, j)) for i in rows for j in range(NX) if last_col(i, j) > 0 and reaches(b, last_col(i, j))]

    def shift_x(by, cores):
        return [
            (at(i, k, j), at(i, k, (j + by) % NX))
            for i in rows
            if i % 2 in cores
            for k in range(NZ)
            for j in range(NX)
            if len(cores) == 1 or NX * k <= last_col(i, 2)
        ]

    def along_y(a, b):
        return [(at(2 * a, k, j), at(2 * b, k, j)) for k in range(NZ) for j in range(NX) if k + j > 0]

    across = [(at(i, k, j), at(i + 1, k, j)) for i in rows[::2] for k in range(NZ) for j in range(NX)]

    def factor_y(a, b):
        return [(at(2 * a + 1, HOME_Z, j), at(2 * b + 1, HOME_Z, j)) for j in range(NX)]

    def factor_z(a, b):
        return [(at(i, (a + HOME_Z) % NZ, j), at(i, (b + HOME_Z) % NZ, j)) for i in rows[1::2] for j in range(NX)]

    home = at(HOME_ROW, HOME_Z, 0)
    home_z = (z - HOME_Z + NZ) % NZ

    def by_x(values):
        return jnp.where(x == 0, values[0], jnp.where(x == 1, values[1], jnp.where(x == 2, values[2], values[3])))

    b_tile = cov[0 : 4 * TB]
    corner = send(b_tile, [(0, home)])
    quarter = [cov[quarter_rows * q : quarter_rows * (q + 1)] for q in range(4)]
    got = [send(quarter[q], scatter(q)) for q in (3, 2, 1)]
    moved = ring_sends(b_tile, FEWER[0], along_y)
    corner, got, moved = tied(corner, got, moved)
    own = by_x([quarter[0], got[2], got[1], got[0]])
    got = ring_sends(own, ROUNDS[0], along_z)
    b_tile = ring_pick(b_tile, FEWER[0], y, moved)
    moved = ring_sends(b_tile, FEWER[1], along_y)

    corner, got = tied(corner, got)
    f = factor_tile(flag, corner)
    f, got, moved = tied(f, got, moved)
    own = ring_pick(own, ROUNDS[0], z, got)
    got = ring_sends(own, ROUNDS[1], along_z)
    b_tile = ring_pick(b_tile, FEWER[1], y, moved)
    moved = ring_sends(b_tile, FEWER[2], along_y)

    part = [f[3 * SB * q : 3 * SB * (q + 1)] for q in range(4)]
    mine = by_x([part[0]] + [send(part[q], [(home, home + q)]) for q in (1, 2, 3)])
    mine = ring_round(mine, ROUNDS[0], y, factor_y)
    mine = ring_round(mine, ROUNDS[1], y, factor_y)

    mine, got, moved = tied(mine, got, moved)
    b_tile = ring_pick(b_tile, FEWER[2], y, moved)
    b_other = send(b_tile, across)
    own = ring_pick(own, ROUNDS[1], z, got)
    left = send(own, shift_x(1, (0, 1)))
    right = send(own, shift_x(-1, (0, 1)))
    mine = ring_round(mine, ROUNDS[0], home_z, factor_z)

    mine, left, right = tied(mine, left, right)
    opp_a = send(left[: quarter_rows // 2], shift_x(1, (0, 1)))
    opp_b = send(right[quarter_rows // 2 :], shift_x(-1, (0, 1)))
    mine = ring_round(mine, ROUNDS[1], home_z, factor_z)

    mine, opp_a, opp_b, b_other = tied(mine, opp_a, opp_b, b_other)
    turned = jnp.concatenate([mine] + [send(mine, shift_x(-by, (1,))) for by in (1, 2, 3)], axis=0)
    turned_other = send(turned, [(b, a) for a, b in across])

    pos = jnp.stack([row, col, x, core]).astype(jnp.int32)
    out = update(pos, own, left, right, opp_a, opp_b, b_tile, b_other, turned, turned_other, cov)
    return out.reshape(covariance.shape)


def solution(mesh):
    return jax.shard_map(
        on_device,
        mesh=mesh,
        in_specs=(P(None, "row", None, "col"),),
        out_specs=P(None, "row", None, "col"),
        check_vma=False,
    )
```

```python
import jax
import jax.numpy as jnp
from jax import lax
from jax.experimental import pallas as pl
from jax.experimental.pallas import tpu as pltpu
from jax.sharding import PartitionSpec as P

AXES = ("row", "col")
ROWS, COLS = 16, 32
NZ, NX = 8, 4
HOME_ROW, HOME_Z = 1, 7
TB = 512
SB = 128
HB = 256
SLOTS = 12
HIGHEST = lax.Precision.HIGHEST
M0, M1, X10, L20, L21, L30, L31, M2, M3, X32 = range(10)


def nn(a, b):
    return lax.dot_general(a, b, (((1,), (0,)), ((), ())), precision=HIGHEST, preferred_element_type=jnp.float32)


def nt(a, b):
    return lax.dot_general(a, b, (((1,), (1,)), ((), ())), precision=HIGHEST, preferred_element_type=jnp.float32)


def factor_block(block):
    tiles = SB // 8
    lane = lax.broadcasted_iota(jnp.int32, (8, SB), 1)
    sub = lax.broadcasted_iota(jnp.int32, (8, SB), 0)
    s = [block[8 * t : 8 * t + 8, :] for t in range(tiles)]
    e = [jnp.where(lane == sub + 8 * t, 1.0, 0.0).astype(jnp.float32) for t in range(tiles)]
    inverse = []
    for b in range(tiles):
        cols = [
            [jnp.broadcast_to(s[t][:, 8 * b + m : 8 * b + m + 1], (8, SB)) for t in range(b, tiles)]
            for m in range(8)
        ]
        top, top_e = s[b], e[b]
        out_e = jnp.zeros_like(top)
        done = []
        for m in range(8):
            d = jnp.broadcast_to(cols[m][0][m : m + 1, :], (8, SB))
            r = lax.rsqrt(d)
            lc = [c * r for c in cols[m]]
            ur = jnp.broadcast_to(top[m : m + 1, :], (8, SB)) * r
            er = jnp.broadcast_to(top_e[m : m + 1, :], (8, SB)) * r
            out_e = jnp.where(sub == m, er, out_e)
            for k in range(m + 1, 8):
                f = jnp.broadcast_to(lc[0][k : k + 1, :], (8, SB))
                cols[k] = [c - l * f for c, l in zip(cols[k], lc)]
            below = jnp.where(sub > m, lc[0], 0.0)
            top = top - below * ur
            top_e = top_e - below * er
            done.append((lc, ur, er))
        for t in range(b + 1, tiles):
            for lc, ur, er in done:
                s[t] = s[t] - lc[t - b] * ur
                e[t] = e[t] - lc[t - b] * er
        inverse.append(out_e)
    return jnp.concatenate(inverse, axis=0)


def wide(ref, first, rows, lo=0, hi=4):
    return jnp.concatenate([ref[pl.ds(4 * first + i, rows, stride=4), :] for i in range(lo, hi)], axis=1)


def put_wide(ref, first, value):
    for i in range(value.shape[1] // SB):
        ref[pl.ds(4 * first + i, value.shape[0], stride=4), :] = value[:, i * SB : (i + 1) * SB]


def factor_kernel(flag_ref, a_ref, f_ref, w_ref):
    @pl.when(flag_ref[0] == 1)
    def _():
        def slot(i):
            return pl.ds(i * SB, SB)

        w_ref[...] = wide(a_ref, 0, TB)
        for k in range(4):
            lo, hi = k * SB, (k + 1) * SB
            inv = factor_block(w_ref[lo:hi, lo:hi])
            f_ref[slot((M0, M1, M2, M3)[k]), :] = inv
            if hi < TB:
                below = nt(w_ref[hi:, lo:hi], inv)
                w_ref[hi:, hi:] = w_ref[hi:, hi:] - nt(below, below)
                w_ref[hi:, lo:hi] = below
                if k < 2:
                    f_ref[slot((L20, L21)[k]), :] = below[2 * SB - hi : 3 * SB - hi]
                    f_ref[slot((L30, L31)[k]), :] = below[3 * SB - hi : 4 * SB - hi]
            if k % 2 == 1:
                prev = f_ref[slot((M0, M2)[k // 2]), :]
                f_ref[slot((X10, X32)[k // 2]), :] = -nn(inv, nn(w_ref[lo:hi, lo - SB : lo], prev))


def factor_tile(flag, a):
    vmem = pl.BlockSpec(memory_space=pltpu.VMEM)
    return pl.pallas_call(
        factor_kernel,
        out_shape=jax.ShapeDtypeStruct((SLOTS * SB, SB), jnp.float32),
        in_specs=[pl.BlockSpec(memory_space=pltpu.SMEM), vmem],
        out_specs=vmem,
        scratch_shapes=[pltpu.VMEM((TB, TB), jnp.float32)],
        cost_estimate=pl.CostEstimate(flops=20_000_000_000, bytes_accessed=3_000_000, transcendentals=0),
        compiler_params=pltpu.CompilerParams(vmem_limit_bytes=24 * 1024 * 1024),
        name="factor",
    )(flag, a)


def update_kernel(
    pos_ref, own_ref, left_ref, right_ref, opp_ref, b_ref, b_other_ref, f_ref, f_other_ref, cov_ref,
    out_ref, y_ref, raw_ref, x_ref,
):
    row, col, x, core = pos_ref[0], pos_ref[1], pos_ref[2], pos_ref[3]
    for shift, ref in ((0, own_ref), (3, left_ref), (1, right_ref), (2, opp_ref)):
        first = lax.rem(x + shift, 4) * HB
        raw_ref[pl.ds(pl.multiple_of(first, HB), HB), :] = wide(ref, 0, HB)

    def block(i):
        place = lax.rem(i // 3 - x + 4, 4)
        rows = pl.ds(pl.multiple_of(place * (3 * SB) + (i % 3) * SB, SB), SB)
        return jnp.where(core == 0, f_other_ref[rows, :], f_ref[rows, :])

    def b_rows(first):
        return jnp.where(core == 1, wide(b_other_ref, first, HB), wide(b_ref, first, HB))

    zero = jnp.zeros((SB, SB), jnp.float32)

    def square(a, b, c, d):
        return jnp.concatenate(
            [jnp.concatenate([a, b], axis=1), jnp.concatenate([c, d], axis=1)], axis=0
        )

    d0 = square(block(M0), zero, block(X10), block(M1))
    d1 = square(block(M2), zero, block(X32), block(M3))
    g = square(block(L20), block(L21), block(L30), block(L31))
    x0 = nt(raw_ref[:, 0:HB], d0)
    x_ref[:, 0:HB] = x0
    x_ref[:, HB:TB] = nt(raw_ref[:, HB:TB] - nt(x0, g), d1)

    @pl.when(col > 0)
    def _():
        y0 = nn(d0, b_rows(0))
        y_ref[0:HB, :] = y0
        y_ref[HB:TB, :] = nn(d1, b_rows(HB) - nn(g, y0))
        prod = nn(x_ref[...], y_ref[...])
        for half in range(2):
            cov = wide(cov_ref, half * TB, TB)
            new = cov - prod[half * TB : (half + 1) * TB]
            put_wide(out_ref, half * TB, jnp.where(row + ROWS * half >= col, new, cov))

    @pl.when(col == 0)
    def _():
        above = lax.broadcasted_iota(jnp.int32, (TB, TB), 1) > lax.broadcasted_iota(jnp.int32, (TB, TB), 0)
        put_wide(out_ref, 0, jnp.where(jnp.logical_and(row == 0, above), 0.0, x_ref[0:TB, :]))
        put_wide(out_ref, TB, x_ref[TB:, :])


def update(*operands):
    vmem = pl.BlockSpec(memory_space=pltpu.VMEM)
    return pl.pallas_call(
        update_kernel,
        out_shape=jax.ShapeDtypeStruct((8 * TB, SB), jnp.float32),
        in_specs=[pl.BlockSpec(memory_space=pltpu.SMEM)] + [vmem] * (len(operands) - 1),
        out_specs=vmem,
        scratch_shapes=[pltpu.VMEM((rows, TB), jnp.float32) for rows in (TB, 2 * TB, 2 * TB)],
        cost_estimate=pl.CostEstimate(flops=8_000_000_000, bytes_accessed=9_000_000, transcendentals=0),
        compiler_params=pltpu.CompilerParams(vmem_limit_bytes=40 * 1024 * 1024),
        name="update",
    )(*operands)


def send(value, pairs):
    return lax.ppermute(value, AXES, pairs)


def one_of(pos, places):
    found = pos == places[0]
    for place in places[1:]:
        found = jnp.logical_or(found, pos == place)
    return found


ROUNDS = (
    (((0, 3),), ((0, 5),)),
    (((0, 1), (3, 4), (5, 6)), ((0, 7), (3, 2))),
)


FEWER = (
    (((0, 4),),),
    (((0, 1), (4, 5)), ((0, 7), (4, 3))),
    (((1, 2), (5, 6)),),
)


def ring_sends(value, moves, lift):
    return [send(value, [p for a, b in pairs for p in lift(a, b)]) for pairs in moves]


def ring_pick(value, moves, pos, got):
    for pairs, received in zip(moves, got):
        value = jnp.where(one_of(pos, [b for _, b in pairs]), received, value)
    return value


def ring_round(value, moves, pos, lift):
    return ring_pick(value, moves, pos, ring_sends(value, moves, lift))


def last_col(row, quarter):
    return row if quarter < 2 else row + ROWS


CHILDREN = {0: (3, 5, 1, 7), 3: (2, 4), 5: (6,), 1: (), 2: (), 4: (), 6: (), 7: ()}


def reaches(place, last):
    return NX * place <= last or any(reaches(c, last) for c in CHILDREN[place])


def on_device(covariance):
    row = lax.axis_index("row")
    col = lax.axis_index("col")
    y, core = row // 2, row % 2
    z, x = col // NX, col % NX
    cov = covariance.reshape(8 * TB, SB)
    flag = jnp.logical_and(row == HOME_ROW, col == HOME_Z * NX).astype(jnp.int32).reshape(1)
    rows = range(ROWS)
    quarter_rows = HB * 4

    def at(i, k, j):
        return i * COLS + k * NX + j

    def tied(*values):
        return lax.optimization_barrier(values)

    def scatter(q):
        return [(at(i, 0, 0), at(i, 0, q)) for i in rows]

    def along_z(a, b):
        return [(at(i, a, j), at(i, b, j)) for i in rows for j in range(NX) if last_col(i, j) > 0 and reaches(b, last_col(i, j))]

    def shift_x(by, cores):
        return [
            (at(i, k, j), at(i, k, (j + by) % NX))
            for i in rows
            if i % 2 in cores
            for k in range(NZ)
            for j in range(NX)
            if len(cores) == 1 or NX * k <= last_col(i, 2)
        ]

    def along_y(a, b):
        return [(at(2 * a, k, j), at(2 * b, k, j)) for k in range(NZ) for j in range(NX) if k + j > 0]

    across = [(at(i, k, j), at(i + 1, k, j)) for i in rows[::2] for k in range(NZ) for j in range(NX)]

    def factor_y(a, b):
        return [(at(2 * a + 1, HOME_Z, j), at(2 * b + 1, HOME_Z, j)) for j in range(NX)]

    def factor_z(a, b):
        return [(at(i, (a + HOME_Z) % NZ, j), at(i, (b + HOME_Z) % NZ, j)) for i in rows[1::2] for j in range(NX)]

    home = at(HOME_ROW, HOME_Z, 0)
    home_z = (z - HOME_Z + NZ) % NZ

    def by_x(values):
        return jnp.where(x == 0, values[0], jnp.where(x == 1, values[1], jnp.where(x == 2, values[2], values[3])))

    b_tile = cov[0 : 4 * TB]
    corner = send(b_tile, [(0, home)])
    quarter = [cov[quarter_rows * q : quarter_rows * (q + 1)] for q in range(4)]
    got = [send(quarter[q], scatter(q)) for q in (3, 2, 1)]
    moved = ring_sends(b_tile, FEWER[0], along_y)
    corner, got, moved = tied(corner, got, moved)
    own = by_x([quarter[0], got[2], got[1], got[0]])
    got = ring_sends(own, ROUNDS[0], along_z)
    b_tile = ring_pick(b_tile, FEWER[0], y, moved)
    moved = ring_sends(b_tile, FEWER[1], along_y)

    corner, got = tied(corner, got)
    f = factor_tile(flag, corner)
    f, got, moved = tied(f, got, moved)
    own = ring_pick(own, ROUNDS[0], z, got)
    got = ring_sends(own, ROUNDS[1], along_z)
    b_tile = ring_pick(b_tile, FEWER[1], y, moved)
    moved = ring_sends(b_tile, FEWER[2], along_y)

    part = [f[3 * SB * q : 3 * SB * (q + 1)] for q in range(4)]
    mine = by_x([part[0]] + [send(part[q], [(home, home + q)]) for q in (1, 2, 3)])
    mine = ring_round(mine, ROUNDS[0], y, factor_y)
    mine = ring_round(mine, ROUNDS[1], y, factor_y)

    mine, got, moved = tied(mine, got, moved)
    own = ring_pick(own, ROUNDS[1], z, got)
    left = send(own, shift_x(1, (0, 1)))
    right = send(own, shift_x(-1, (0, 1)))
    opposite = send(own, shift_x(2, (0, 1)))
    mine = ring_round(mine, ROUNDS[0], home_z, factor_z)
    mine = ring_round(mine, ROUNDS[1], home_z, factor_z)

    mine, left, right, opposite, moved = tied(mine, left, right, opposite, moved)
    b_tile = ring_pick(b_tile, FEWER[2], y, moved)
    b_other = send(b_tile, across)
    turned = jnp.concatenate([mine] + [send(mine, shift_x(-by, (1,))) for by in (1, 2, 3)], axis=0)
    turned_other = send(turned, [(b, a) for a, b in across])

    pos = jnp.stack([row, col, x, core]).astype(jnp.int32)
    out = update(pos, own, left, right, opposite, b_tile, b_other, turned, turned_other, cov)
    return out.reshape(covariance.shape)


def solution(mesh):
    return jax.shard_map(
        on_device,
        mesh=mesh,
        in_specs=(P(None, "row", None, "col"),),
        out_specs=P(None, "row", None, "col"),
        check_vma=False,
    )
```

```python
import jax
import jax.numpy as jnp
from jax import lax
from jax.experimental import pallas as pl
from jax.experimental.pallas import tpu as pltpu
from jax.sharding import PartitionSpec as P

AXES = ("row", "col")
ROWS, COLS = 16, 32
NZ, NX = 8, 4
HOME_ROW, HOME_Z = 1, 7
TB = 512
SB = 128
HB = 256
SLOTS = 12
HIGHEST = lax.Precision.HIGHEST
M0, M1, X10, L20, L21, L30, L31, M2, M3, X32 = range(10)


def nn(a, b):
    return lax.dot_general(a, b, (((1,), (0,)), ((), ())), precision=HIGHEST, preferred_element_type=jnp.float32)


def nt(a, b):
    return lax.dot_general(a, b, (((1,), (1,)), ((), ())), precision=HIGHEST, preferred_element_type=jnp.float32)


def factor_block(block):
    tiles = SB // 8
    lane = lax.broadcasted_iota(jnp.int32, (8, SB), 1)
    sub = lax.broadcasted_iota(jnp.int32, (8, SB), 0)
    s = [block[8 * t : 8 * t + 8, :] for t in range(tiles)]
    e = [jnp.where(lane == sub + 8 * t, 1.0, 0.0).astype(jnp.float32) for t in range(tiles)]
    inverse = []
    for b in range(tiles):
        cols = [
            [jnp.broadcast_to(s[t][:, 8 * b + m : 8 * b + m + 1], (8, SB)) for t in range(b, tiles)]
            for m in range(8)
        ]
        top, top_e = s[b], e[b]
        out_e = jnp.zeros_like(top)
        done = []
        for m in range(8):
            d = jnp.broadcast_to(cols[m][0][m : m + 1, :], (8, SB))
            r = lax.rsqrt(d)
            lc = [c * r for c in cols[m]]
            ur = jnp.broadcast_to(top[m : m + 1, :], (8, SB)) * r
            er = jnp.broadcast_to(top_e[m : m + 1, :], (8, SB)) * r
            out_e = jnp.where(sub == m, er, out_e)
            for k in range(m + 1, 8):
                f = jnp.broadcast_to(lc[0][k : k + 1, :], (8, SB))
                cols[k] = [c - l * f for c, l in zip(cols[k], lc)]
            below = jnp.where(sub > m, lc[0], 0.0)
            top = top - below * ur
            top_e = top_e - below * er
            done.append((lc, ur, er))
        for t in range(b + 1, tiles):
            for lc, ur, er in done:
                s[t] = s[t] - lc[t - b] * ur
                e[t] = e[t] - lc[t - b] * er
        inverse.append(out_e)
    return jnp.concatenate(inverse, axis=0)


def wide(ref, first, rows, lo=0, hi=4):
    return jnp.concatenate([ref[pl.ds(4 * first + i, rows, stride=4), :] for i in range(lo, hi)], axis=1)


def put_wide(ref, first, value):
    for i in range(value.shape[1] // SB):
        ref[pl.ds(4 * first + i, value.shape[0], stride=4), :] = value[:, i * SB : (i + 1) * SB]


def factor_kernel(flag_ref, a_ref, f_ref, w_ref):
    @pl.when(flag_ref[0] == 1)
    def _():
        def slot(i):
            return pl.ds(i * SB, SB)

        w_ref[...] = wide(a_ref, 0, TB)
        for k in range(4):
            lo, hi = k * SB, (k + 1) * SB
            inv = factor_block(w_ref[lo:hi, lo:hi])
            f_ref[slot((M0, M1, M2, M3)[k]), :] = inv
            if hi < TB:
                below = nt(w_ref[hi:, lo:hi], inv)
                w_ref[hi:, hi:] = w_ref[hi:, hi:] - nt(below, below)
                w_ref[hi:, lo:hi] = below
                if k < 2:
                    f_ref[slot((L20, L21)[k]), :] = below[2 * SB - hi : 3 * SB - hi]
                    f_ref[slot((L30, L31)[k]), :] = below[3 * SB - hi : 4 * SB - hi]
            if k % 2 == 1:
                prev = f_ref[slot((M0, M2)[k // 2]), :]
                f_ref[slot((X10, X32)[k // 2]), :] = -nn(inv, nn(w_ref[lo:hi, lo - SB : lo], prev))


def factor_tile(flag, a):
    vmem = pl.BlockSpec(memory_space=pltpu.VMEM)
    return pl.pallas_call(
        factor_kernel,
        out_shape=jax.ShapeDtypeStruct((SLOTS * SB, SB), jnp.float32),
        in_specs=[pl.BlockSpec(memory_space=pltpu.SMEM), vmem],
        out_specs=vmem,
        scratch_shapes=[pltpu.VMEM((TB, TB), jnp.float32)],
        cost_estimate=pl.CostEstimate(flops=20_000_000_000, bytes_accessed=3_000_000, transcendentals=0),
        compiler_params=pltpu.CompilerParams(vmem_limit_bytes=24 * 1024 * 1024),
        name="factor",
    )(flag, a)


def update_kernel(
    pos_ref, own_ref, left_ref, right_ref, opp_ref, b_ref, b_other_ref, f_ref, f_other_ref, cov_ref,
    out_ref, y_ref, raw_ref, x_ref,
):
    row, col, x, core = pos_ref[0], pos_ref[1], pos_ref[2], pos_ref[3]
    for shift, ref in ((0, own_ref), (3, left_ref), (1, right_ref), (2, opp_ref)):
        first = lax.rem(x + shift, 4) * HB
        raw_ref[pl.ds(pl.multiple_of(first, HB), HB), :] = wide(ref, 0, HB)

    def block(i):
        place = lax.rem(i // 3 - x + 4, 4)
        rows = pl.ds(pl.multiple_of(place * (3 * SB) + (i % 3) * SB, SB), SB)
        return jnp.where(core == 0, f_other_ref[rows, :], f_ref[rows, :])

    def b_rows(first):
        return jnp.where(core == 1, wide(b_other_ref, first, HB), wide(b_ref, first, HB))

    zero = jnp.zeros((SB, SB), jnp.float32)

    def square(a, b, c, d):
        return jnp.concatenate(
            [jnp.concatenate([a, b], axis=1), jnp.concatenate([c, d], axis=1)], axis=0
        )

    d0 = square(block(M0), zero, block(X10), block(M1))
    d1 = square(block(M2), zero, block(X32), block(M3))
    g = square(block(L20), block(L21), block(L30), block(L31))
    x0 = nt(raw_ref[:, 0:HB], d0)
    x_ref[:, 0:HB] = x0
    x_ref[:, HB:TB] = nt(raw_ref[:, HB:TB] - nt(x0, g), d1)

    @pl.when(col > 0)
    def _():
        y0 = nn(d0, b_rows(0))
        y_ref[0:HB, :] = y0
        y_ref[HB:TB, :] = nn(d1, b_rows(HB) - nn(g, y0))
        prod = nn(x_ref[...], y_ref[...])
        for half in range(2):
            cov = wide(cov_ref, half * TB, TB)
            new = cov - prod[half * TB : (half + 1) * TB]
            put_wide(out_ref, half * TB, jnp.where(row + ROWS * half >= col, new, cov))

    @pl.when(col == 0)
    def _():
        above = lax.broadcasted_iota(jnp.int32, (TB, TB), 1) > lax.broadcasted_iota(jnp.int32, (TB, TB), 0)
        put_wide(out_ref, 0, jnp.where(jnp.logical_and(row == 0, above), 0.0, x_ref[0:TB, :]))
        put_wide(out_ref, TB, x_ref[TB:, :])


def update(*operands):
    vmem = pl.BlockSpec(memory_space=pltpu.VMEM)
    return pl.pallas_call(
        update_kernel,
        out_shape=jax.ShapeDtypeStruct((8 * TB, SB), jnp.float32),
        in_specs=[pl.BlockSpec(memory_space=pltpu.SMEM)] + [vmem] * (len(operands) - 1),
        out_specs=vmem,
        scratch_shapes=[pltpu.VMEM((rows, TB), jnp.float32) for rows in (TB, 2 * TB, 2 * TB)],
        cost_estimate=pl.CostEstimate(flops=8_000_000_000, bytes_accessed=9_000_000, transcendentals=0),
        compiler_params=pltpu.CompilerParams(vmem_limit_bytes=40 * 1024 * 1024),
        name="update",
    )(*operands)


def send(value, pairs):
    return lax.ppermute(value, AXES, pairs)


def one_of(pos, places):
    found = pos == places[0]
    for place in places[1:]:
        found = jnp.logical_or(found, pos == place)
    return found


ROUNDS = (
    (((0, 3),), ((0, 5),)),
    (((0, 1), (3, 4), (5, 6)), ((0, 7), (3, 2))),
)


FEWER = (
    (((0, 4),),),
    (((0, 1), (4, 5)), ((0, 7), (4, 3))),
    (((1, 2), (5, 6)),),
)


def ring_sends(value, moves, lift):
    return [send(value, [p for a, b in pairs for p in lift(a, b)]) for pairs in moves]


def ring_pick(value, moves, pos, got):
    for pairs, received in zip(moves, got):
        value = jnp.where(one_of(pos, [b for _, b in pairs]), received, value)
    return value


def ring_round(value, moves, pos, lift):
    return ring_pick(value, moves, pos, ring_sends(value, moves, lift))


def last_col(row, quarter):
    return row if quarter < 2 else row + ROWS


CHILDREN = {0: (3, 5, 1, 7), 3: (2, 4), 5: (6,), 1: (), 2: (), 4: (), 6: (), 7: ()}


def reaches(place, last):
    return NX * place <= last or any(reaches(c, last) for c in CHILDREN[place])


def on_device(covariance):
    row = lax.axis_index("row")
    col = lax.axis_index("col")
    y, core = row // 2, row % 2
    z, x = col // NX, col % NX
    cov = covariance.reshape(8 * TB, SB)
    flag = jnp.logical_and(row == HOME_ROW, col == HOME_Z * NX).astype(jnp.int32).reshape(1)
    rows = range(ROWS)
    quarter_rows = HB * 4

    def at(i, k, j):
        return i * COLS + k * NX + j

    def tied(*values):
        return lax.optimization_barrier(values)

    def scatter(q):
        return [(at(i, 0, 0), at(i, 0, q)) for i in rows]

    def along_z(a, b):
        return [(at(i, a, j), at(i, b, j)) for i in rows for j in range(NX) if last_col(i, j) > 0 and reaches(b, last_col(i, j))]

    def shift_x(by, cores):
        return [
            (at(i, k, j), at(i, k, (j + by) % NX))
            for i in rows
            if i % 2 in cores
            for k in range(NZ)
            for j in range(NX)
            if len(cores) == 1 or NX * k <= last_col(i, 2)
        ]

    def along_y(a, b):
        return [(at(2 * a, k, j), at(2 * b, k, j)) for k in range(NZ) for j in range(NX) if k + j > 0]

    across = [(at(i, k, j), at(i + 1, k, j)) for i in rows[::2] for k in range(NZ) for j in range(NX)]

    def factor_y(a, b):
        return [(at(2 * a + 1, HOME_Z, j), at(2 * b + 1, HOME_Z, j)) for j in range(NX)]

    def factor_z(a, b):
        return [(at(i, (a + HOME_Z) % NZ, j), at(i, (b + HOME_Z) % NZ, j)) for i in rows[1::2] for j in range(NX)]

    home = at(HOME_ROW, HOME_Z, 0)
    home_z = (z - HOME_Z + NZ) % NZ

    def by_x(values):
        return jnp.where(x == 0, values[0], jnp.where(x == 1, values[1], jnp.where(x == 2, values[2], values[3])))

    b_tile = cov[0 : 4 * TB]
    corner = send(b_tile, [(0, home)])
    quarter = [cov[quarter_rows * q : quarter_rows * (q + 1)] for q in range(4)]
    got = [send(quarter[q], scatter(q)) for q in (3, 2, 1)]
    moved = ring_sends(b_tile, FEWER[0], along_y)
    corner, got, moved = tied(corner, got, moved)
    own = by_x([quarter[0], got[2], got[1], got[0]])
    got = ring_sends(own, ROUNDS[0], along_z)
    b_tile = ring_pick(b_tile, FEWER[0], y, moved)
    moved = ring_sends(b_tile, FEWER[1], along_y)

    corner, got = tied(corner, got)
    f = factor_tile(flag, corner)
    f, got, moved = tied(f, got, moved)
    own = ring_pick(own, ROUNDS[0], z, got)
    got = ring_sends(own, ROUNDS[1], along_z)
    b_tile = ring_pick(b_tile, FEWER[1], y, moved)
    moved = ring_sends(b_tile, FEWER[2], along_y)

    part = [f[3 * SB * q : 3 * SB * (q + 1)] for q in range(4)]
    mine = by_x([part[0]] + [send(part[q], [(home, home + q)]) for q in (1, 2, 3)])
    mine = ring_round(mine, ROUNDS[0], y, factor_y)
    mine = ring_round(mine, ROUNDS[1], y, factor_y)

    mine, got, moved = tied(mine, got, moved)
    own = ring_pick(own, ROUNDS[1], z, got)
    left = send(own, shift_x(1, (0, 1)))
    right = send(own, shift_x(-1, (0, 1)))
    opposite = send(own, shift_x(2, (0, 1)))
    mine = ring_round(mine, ROUNDS[0], home_z, factor_z)
    mine = ring_round(mine, ROUNDS[1], home_z, factor_z)

    mine, moved = tied(mine, moved)
    b_tile = ring_pick(b_tile, FEWER[2], y, moved)
    b_other = send(b_tile, across)
    mine, left, right, opposite, b_other = tied(mine, left, right, opposite, b_other)
    turned = jnp.concatenate([mine] + [send(mine, shift_x(-by, (1,))) for by in (1, 2, 3)], axis=0)
    turned_other = send(turned, [(b, a) for a, b in across])

    pos = jnp.stack([row, col, x, core]).astype(jnp.int32)
    out = update(pos, own, left, right, opposite, b_tile, b_other, turned, turned_other, cov)
    return out.reshape(covariance.shape)


def solution(mesh):
    return jax.shard_map(
        on_device,
        mesh=mesh,
        in_specs=(P(None, "row", None, "col"),),
        out_specs=P(None, "row", None, "col"),
        check_vma=False,
    )
```
